256 devices in a mesh: req: 32 (over y, z), head: 2 (over core), grp: 4 (over x).
Axes of the slice: x: 4, y: 4, z: 8, core: 2. Of those that a mesh axis runs over, the one named last changes fastest.
Arguments:
- residual: bfloat16 [1024, 7168], P(('req', 'grp'), 'head'), may hold values from -12 to 12
- attn_part: bfloat16 [2, 1024, 7168], P('head', ('req', 'grp')), may hold values from -6 to 6
- norm_gain: float32 [7168], P('head'), may hold values from 0.1 to 1.9
- routes: int32 [1024, 8], P(('req', 'grp')), may hold values from 0 to 31, all different within a row; in each aligned block of 8 rows (0 to 7, 8 to 15, ...) at most 4 rows name the same one
- gates: float32 [1024, 8], P(('req', 'grp')), may hold values from 0.1 to 0.6
- gate_weight: bfloat16 [32, 7168, 2048], P('req', None, ('head', 'grp')), may hold values from -0.0625 to 0.0625
- up_weight: bfloat16 [32, 7168, 2048], P('req', None, ('head', 'grp')), may hold values from -0.0625 to 0.0625
- down_weight: bfloat16 [32, 2048, 7168], P('req', None, ('head', 'grp')), may hold values from -0.125 to 0.125
Outputs:
- mixed: bfloat16 [1024, 7168], P(('req', 'grp'), 'head')
The draws below stay inside these ranges and needn't reach their ends.
Inputs may be any that keep to these rules, and one draw needn't show every extreme that they name: `routes`: each row names 8 different experts. In each aligned block of 8 rows (the rows of one index pair of req and grp) no expert is named more than 4 times, a bound that some block reaches.
All inputs are finite; a program needn't handle non-finite values.
Results may differ from the reference program's by a relative error of at most 0.012.
Values may be sent and summed in bfloat16 or wider, within the bound.
A program may use at most 128 MiB of HBM per device.

```python
import math
import jax
import jax.numpy as jnp
import numpy as np
from jax import lax

D = 7168
FF = 2048
TOP = 8
EXPERTS = 32
TOK_DEV = 8
CAP = 4
TOKENS = 1024


def draw_residual(key, part):
    key = jax.random.fold_in(key, 11)
    columns = jnp.arange(D)
    values = jax.random.normal(key, (TOKENS, D), jnp.float32)
    scale = jnp.where(columns < D // 2, 0.4, 2.0)
    return jnp.clip(values * scale[None, :], -12.0, 12.0).astype(jnp.bfloat16)


def with_spikes(drawn, own_key, source, target, blocks, factor):
    owner, partner = [(jnp.arange(drawn.shape[dim]) // (drawn.shape[dim] // blocks)).reshape([-1 if axis == dim else 1 for axis in range(drawn.ndim)]) for dim in (source, target)]
    chosen = jax.random.permutation(own_key, blocks)[partner]
    strong = (owner == chosen) | (owner == (partner + blocks // 2) % blocks)
    return jnp.where(strong, factor * drawn, drawn)


def levels(stream_key, dims, shards, low, top_value):
    def one(dim, blocks):
        heights = jax.random.uniform(jax.random.fold_in(jax.random.fold_in(stream_key, 6), dim), (blocks,), jnp.float32, low / len(shards), top_value / len(shards))
        return jnp.repeat(jnp.exp(heights), dims[dim] // blocks).reshape((-1,) + (1,) * (len(dims) - dim - 1))

    level = one(*shards[0])
    for cut in shards[1:]:
        level = level * one(*cut)
    return level


def deal_out(rng, own, number, rows, count, top, bound, lean):
    ranking = jax.random.permutation(rng, count)
    crowded, usual = shares(count, rows * top, bound, lean, True), shares(count, rows * top, bound, lean, False)
    places = jnp.arange(count)

    def named(tallies, turn):
        used = int((tallies > 0).sum())
        fixed = max(1, used // 4)
        moved = fixed + (places - fixed + turn * (used - fixed)) % max(1, count - fixed)
        return jnp.zeros((count,), jnp.int32).at[ranking[jnp.where(places < fixed, places, moved)]].set(jnp.asarray(tallies, jnp.int32))

    tallies = jnp.where(number % 4 == 0, named(crowded, number // 4), named(usual, number - number // 4 - 1))
    mixed = jax.random.permutation(jax.random.fold_in(own, 3), count)
    donor, sink = mixed[0:count // 2 * 2:2], mixed[1:count // 2 * 2:2]
    margin = jnp.minimum(tallies[donor] - 1, bound - tallies[sink]) // 2
    margin = jnp.where((donor == ranking[0]) | (sink == ranking[0]) | (tallies[sink] == 0), 0, jnp.maximum(margin, 0))
    moved = jax.random.randint(jax.random.fold_in(own, 4), (count // 2,), 0, 1 << 20) % (margin + 1)
    tallies = tallies.at[donor].add(-moved).at[sink].add(moved)
    items = jnp.searchsorted(jnp.cumsum(tallies), jnp.arange(rows * top), side="right").astype(jnp.int32)
    table = items.reshape(top, rows).T
    table = table[jax.random.permutation(jax.random.fold_in(own, 1), rows)]
    turn = jax.random.randint(jax.random.fold_in(own, 2), (rows, 1), 0, top)
    return jnp.take_along_axis(table, (jnp.arange(top)[None, :] + turn) % top, axis=1)


def shares(amount, total, reach, slope, full):
    loads = [(1 << 20) // math.isqrt(standing ** slope) + 1 for standing in range(1, amount + 1)]
    largest = reach if full else min(reach, max(-(-total // amount), total * loads[0] // sum(loads)))
    least = 1 if total - largest >= amount - 1 else 0
    counts, rest = [largest] + [least] * (amount - 1), total - largest - least * (amount - 1)
    while rest > 0:
        movable = [i for i in range(1, amount) if counts[i] < largest] or [i for i in range(1, amount) if counts[i] < reach]
        pool, left = sum([loads[i] for i in movable]), rest
        for i in movable:
            more = min(reach - counts[i], max(1, left * loads[i] // pool), rest)
            counts[i] = counts[i] + more
            rest = rest - more
    return np.array(counts)


def normal_values(key, shape, scale, reach, cuts=(), held_as=jnp.bfloat16):
    gain = levels(key, shape, cuts, -0.22, 0.18) if cuts else 1.0
    drawn = jax.random.normal(key, shape, jnp.float32) * scale * gain
    return jnp.minimum(jnp.maximum(drawn, -reach), reach).astype(held_as)


def heavy_noise(own_key, dims, deviation, limit, cuts, heavy, kind=jnp.bfloat16):
    drawn = deviation * jax.random.normal(own_key, dims, jnp.float32)
    if cuts:
        drawn = drawn * levels(own_key, dims, cuts, -0.22, 0.18)
    return jnp.clip(with_spikes(drawn, jax.random.fold_in(own_key, 3), *heavy), -limit, limit).astype(kind)


def setup_inputs(seed: int = 0) -> dict:
    keys = jax.random.split(jax.random.key(seed), 9)
    residual = draw_residual(jax.random.fold_in(keys[8], 71), 0)
    attn_part = heavy_noise(keys[1], (2, TOKENS, D), 0.7, 6.0, ((0, 2), (1, 128)), (0, 2, 2, 2.0))
    norm_gain = jnp.clip(1.0 + 0.18 * jax.random.normal(keys[2], (D,), jnp.float32), 0.1, 1.9)
    routes_keys = jax.random.split(jax.random.fold_in(keys[3], 1), TOKENS // TOK_DEV)
    routes_turns = jax.random.permutation(jax.random.fold_in(keys[3], 3), TOKENS // TOK_DEV)
    routes = jax.vmap(lambda own, number: deal_out(jax.random.fold_in(keys[3], 2), own, number, TOK_DEV, EXPERTS, TOP, CAP, 2))(routes_keys, routes_turns).reshape((TOKENS, TOP))
    gates = jnp.clip(0.1 + 0.5 * jax.random.uniform(keys[4], (TOKENS, TOP), jnp.float32) ** levels(keys[4], (TOKENS, TOP), ((0, 128),), -0.2, 0.2), 0.1, 0.6)
    gate_weight = normal_values(keys[5], (EXPERTS, D, FF), D ** -0.5, 0.0625, ((0, 32), (2, 8)))
    up_weight = normal_values(keys[6], (EXPERTS, D, FF), D ** -0.5, 0.0625, ((0, 32), (2, 8)))
    down_weight = normal_values(keys[7], (EXPERTS, FF, D), FF ** -0.5, 0.125, ((0, 32), (2, 8)))
    return dict(residual=residual, attn_part=attn_part, norm_gain=norm_gain, routes=routes, gates=gates, gate_weight=gate_weight, up_weight=up_weight, down_weight=down_weight)


EPSILON = 1e-06

def expert_apply(operands):
    rows_in, weight_gate, weight_up, weight_down = operands
    gate_act = jnp.dot(rows_in, weight_gate, preferred_element_type=jnp.float32)
    up_act = jnp.dot(rows_in, weight_up, preferred_element_type=jnp.float32)
    hidden_units = (jax.nn.silu(gate_act) * up_act).astype(jnp.bfloat16)
    return jnp.dot(hidden_units, weight_down, preferred_element_type=jnp.float32).astype(jnp.bfloat16)

def reference(residual, attn_part, norm_gain, routes, gates, gate_weight, up_weight, down_weight):
    attention = attn_part[0].astype(jnp.float32) + attn_part[1].astype(jnp.float32)
    hidden_state = residual.astype(jnp.float32) + attention
    row_scale = lax.rsqrt(lax.optimization_barrier(jnp.mean(hidden_state * hidden_state, axis=1, keepdims=True)) + EPSILON)
    normed = (hidden_state * row_scale * norm_gain[None, :]).astype(jnp.bfloat16)
    blocks = TOKENS // TOK_DEV
    flat_routes = routes.reshape(blocks, TOK_DEV * TOP)
    onehot = (flat_routes[:, :, None] == jnp.arange(EXPERTS, dtype=jnp.int32)[None, None, :]).astype(jnp.int32)
    earlier = jnp.cumsum(onehot, axis=1) - onehot
    slot_index = lax.optimization_barrier(jnp.sum(earlier * onehot, axis=2)).reshape(TOKENS, TOP).astype(jnp.int32)
    block_index = (jnp.arange(TOKENS, dtype=jnp.int32) // TOK_DEV)[:, None]
    position = (block_index * CAP + slot_index).astype(jnp.int32)
    spread_rows = jnp.broadcast_to(normed[:, None, :], (TOKENS, TOP, D))
    buffer = jnp.zeros((EXPERTS, blocks * CAP, D), jnp.bfloat16).at[routes, position].set(spread_rows)
    outputs = lax.map(expert_apply, (buffer, gate_weight, up_weight, down_weight))
    picked = outputs[routes, position].astype(jnp.float32)
    routed = lax.optimization_barrier(jnp.sum(gates[:, :, None] * picked, axis=1))
    return (hidden_state + routed).astype(jnp.bfloat16)
```

```python
import functools

import jax
import jax.numpy as jnp
from jax import lax
from jax.experimental import pallas as pl
from jax.experimental.pallas import tpu as pltpu
from jax.sharding import PartitionSpec as P

MESH = pl.DeviceIdType.MESH
D = 7168
HALF = D // 2
QUART = HALF // 2
CAP = 4
TOK = 8
NX, NY, NZ = 4, 4, 8
FFS = 256
OUTS = 896
EPSILON = 1e-06

ZREL = (0, 1, 7, 2, 6, 3, 5, 4)
YREL = (0, 1, 3, 2)
ZSLOT = {rel: slot for slot, rel in enumerate(ZREL)}
YSLOT = {rel: slot for slot, rel in enumerate(YREL)}


def kernel(
    res_ref,
    attn_ref,
    gain_ref,
    routes_ref,
    gates_ref,
    wg_hbm,
    wu_hbm,
    wd_hbm,
    out_ref,
    wg,
    wu,
    wd,
    ex,
    hid,
    zb,
    zi,
    xi,
    ysel,
    xb,
    acc,
    hb,
    dacc,
    obs,
    rb,
    fs,
    fb,
    wsem,
    ex_s,
    ex_r,
    zb_s,
    zb_r,
    zi_s,
    zi_r,
    xi_s,
    xi_r,
    y_s,
    y_r,
    xn_s,
    xn_r,
    xf_s,
    xf_r,
    sib_s,
    sib_r,
    h_s,
    h_r,
    hs_s,
    hs_r,
    r_s,
    r_r,
    f_s,
    f_r,
):
    req, h, x = lax.axis_index("req"), lax.axis_index("head"), lax.axis_index("grp")
    y, z = req // NZ, req % NZ

    def dev(dx=0, dy=0, dz=0, sib=False):
        return {
            "req": ((y + dy) % NY) * NZ + (z + dz) % NZ,
            "head": 1 - h if sib else h,
            "grp": (x + dx) % NX,
        }

    sends = []

    def send(src, dst, ssem, rsem, to):
        copy = pltpu.make_async_remote_copy(
            src_ref=src, dst_ref=dst, send_sem=ssem, recv_sem=rsem, device_id=to, device_id_type=MESH
        )
        copy.start()
        sends.append(copy)

    def arrived(dst, ssem, rsem):
        pltpu.make_async_remote_copy(
            src_ref=dst, dst_ref=dst, send_sem=ssem, recv_sem=rsem, device_id=dev(sib=True), device_id_type=MESH
        ).wait_recv()

    loads = [
        pltpu.make_async_copy(src.at[0], dst, wsem.at[i])
        for i, (src, dst) in enumerate(((wg_hbm, wg), (wu_hbm, wu), (wd_hbm, wd)))
    ]
    for load in loads:
        load.start()

    bar = pltpu.get_barrier_semaphore()
    peers = [dev(sib=True)] + [dev(dx=d) for d in range(1, NX)]
    peers += [dev(dy=a, dz=b) for a in range(NY) for b in range(NZ) if a or b]
    for peer in peers:
        pl.semaphore_signal(bar, inc=1, device_id=peer, device_id_type=MESH)

    attn = attn_ref[...].astype(jnp.float32)
    res = res_ref[...].astype(jnp.float32)
    ex[0, :, :HALF] = jnp.concatenate([attn[:, :HALF], attn[:, HALF:]], axis=0).astype(jnp.bfloat16)
    ex[0, :, HALF:] = jnp.concatenate([res[:, :QUART], res[:, QUART:]], axis=0).astype(jnp.bfloat16)

    routes = routes_ref[...]
    gates = gates_ref[...]
    column = lax.broadcasted_iota(jnp.int32, (TOK, 128), 1)
    named = jnp.zeros((TOK, 128), jnp.float32)
    value = jnp.zeros((TOK, 128), jnp.float32)
    for k in range(8):
        hit = (routes[:, k : k + 1] == column // CAP).astype(jnp.float32)
        named = named + hit
        value = value + hit * gates[:, k : k + 1]
    row = lax.broadcasted_iota(jnp.int32, (TOK, 128), 0)
    before = jnp.zeros((TOK, 128), jnp.float32)
    for t in range(TOK - 1):
        before = before + jnp.where(row > t, named[t : t + 1, :], 0.0)
    info = jnp.where(before == (column % CAP).astype(jnp.float32), value, 0.0)
    zi[0] = info
    xi[x] = info

    pl.semaphore_wait(bar, len(peers))
    send(ex.at[0], ex.at[1], ex_s.at[0], ex_r.at[0], dev(sib=True))
    order = [(NZ - ZREL[slot]) % NZ for slot in range(1, NZ)]
    for d in order:
        slot = ZSLOT[(-d) % NZ]
        send(zi.at[0], zi.at[slot], zi_s.at[slot], zi_r.at[slot], dev(dz=d))
    for d in (1, 3, 2):
        send(xi.at[x], xi.at[x], xi_s.at[d], xi_r.at[4 - d], dev(dx=d))

    arrived(ex.at[1], ex_s.at[0], ex_r.at[0])
    theirs = ex[1].astype(jnp.float32)
    t_attn = (theirs[:TOK, :HALF], theirs[TOK:, :HALF])
    m_attn = (attn[:, :HALF], attn[:, HALF:])
    t_res = jnp.concatenate([theirs[:TOK, HALF:], theirs[TOK:, HALF:]], axis=1)
    sums = (m_attn[0] + t_attn[0], m_attn[1] + t_attn[1])
    first = h == 0
    own = res + jnp.where(first, sums[0], sums[1])
    other = t_res + jnp.where(first, sums[1], sums[0])
    squares = jnp.sum(own * own, axis=1, keepdims=True) + jnp.sum(other * other, axis=1, keepdims=True)
    scale = lax.rsqrt(squares / D + EPSILON)
    normed = own * scale * gain_ref[...]
    hid[...] = own
    zb[0] = jnp.concatenate([normed[:, :QUART], normed[:, QUART:]], axis=0).astype(jnp.bfloat16)
    for d in order:
        slot = ZSLOT[(-d) % NZ]
        send(zb.at[0], zb.at[slot], zb_s.at[slot], zb_r.at[slot], dev(dz=d))

    left, right = (x + 3) % NX, (x + 1) % NX

    def x_send(c, yr):
        piece = xb.at[c, h, yr, x]
        send(piece, piece, xn_s.at[c, yr, 0], xn_r.at[c, yr, 0], dev(dx=1))
        send(piece, piece, xn_s.at[c, yr, 1], xn_r.at[c, yr, 1], dev(dx=3))
        send(piece, piece, sib_s.at[c, yr, 0], sib_r.at[c, yr, 0], dev(sib=True))

    def x_forward(c, yr):
        for way, source, to in ((0, left, 1), (1, right, 3)):
            piece = xb.at[c, h, yr, source]
            arrived(piece, xn_s.at[c, yr, way], xn_r.at[c, yr, way])
            part = xb.at[c, h, yr, source, :, pl.ds(way * QUART, QUART)]
            send(part, part, xf_s.at[c, yr, way], xf_r.at[c, yr, way], dev(dx=to))
            send(piece, piece, sib_s.at[c, yr, 1 + way], sib_r.at[c, yr, 1 + way], dev(sib=True))

    def x_far(c, yr):
        far = (x + 2) % NX
        for way in (0, 1):
            part = xb.at[c, h, yr, far, :, pl.ds(way * QUART, QUART)]
            arrived(part, xf_s.at[c, yr, way], xf_r.at[c, yr, way])
        piece = xb.at[c, h, yr, far]
        send(piece, piece, sib_s.at[c, yr, 3], sib_r.at[c, yr, 3], dev(sib=True))

    def sib_wait(c):
        for yr in range(NY):
            for kind, source in enumerate((x, left, right, (x + 2) % NX)):
                piece = xb.at[c, 1 - h, yr, source]
                arrived(piece, sib_s.at[c, yr, kind], sib_r.at[c, yr, kind])

    def y_wait(c, yr):
        piece = xb.at[c, h, yr, x]
        arrived(piece, y_s.at[c, yr], y_r.at[c, yr])

    def select(c):
        for slot in range(4 * c, 4 * c + 4):
            if slot:
                arrived(zi.at[slot], zi_s.at[slot], zi_r.at[slot])
                arrived(zb.at[slot], zb_s.at[slot], zb_r.at[slot])
        tables = [(zi[4 * c + j] != 0.0).astype(jnp.bfloat16) for j in range(4)]
        table = jnp.concatenate([t for j in range(4) for t in (tables[j], tables[j])], axis=0)
        rows16 = lax.broadcasted_iota(jnp.int32, (16, 128), 0) % CAP
        cols16 = lax.broadcasted_iota(jnp.int32, (16, 128), 1)
        pick = jnp.concatenate(
            [
                (cols16 == rows16 + (((y + rel) % NY) * NZ + z) * CAP).astype(jnp.float32)
                for rel in YREL
            ],
            axis=0,
        ).astype(jnp.bfloat16)
        small = lax.dot_general(
            pick, table, (((1,), (1,)), ((), ())), preferred_element_type=jnp.float32
        )
        r = lax.broadcasted_iota(jnp.int32, (64, 64), 0)
        m = lax.broadcasted_iota(jnp.int32, (64, 64), 1)
        blocks = zb[4 * c : 4 * c + 4].reshape(64, QUART)
        for u in (0, 1):
            mask = ((r // 4) % 4 == m // 16) & ((m // 8) % 2 == u)
            onehot = jnp.where(mask, small, 0.0).astype(jnp.bfloat16)
            rows = jnp.dot(onehot, blocks, preferred_element_type=jnp.float32).astype(jnp.bfloat16)
            cols = slice(u * QUART, (u + 1) * QUART)
            xb[c, h, 0, x, :, cols] = rows[:16]
            for yr in range(1, NY):
                ysel[c, yr, :, cols] = rows[16 * yr : 16 * yr + 16]
        for yr in (1, 2, 3):
            back = YSLOT[(-YREL[yr]) % NY]
            send(ysel.at[c, yr], xb.at[c, h, back, x], y_s.at[c, back], y_r.at[c, back], dev(dy=YREL[yr]))
        x_send(c, 0)

    def up(c):
        acc[...] = jnp.zeros_like(acc)

        def step(i, carry):
            part = xb[c, i // 2, :, :, :, pl.ds(pl.multiple_of((i % 2) * QUART, QUART), QUART)]
            rows = part.reshape(256, QUART)
            ks = pl.ds(pl.multiple_of(i * QUART, QUART), QUART)
            acc[:, :FFS] += jnp.dot(rows, wg[ks, :], preferred_element_type=jnp.float32)
            acc[:, FFS:] += jnp.dot(rows, wu[ks, :], preferred_element_type=jnp.float32)
            return carry

        lax.fori_loop(0, 4, step, 0)
        gate = acc[:, :FFS]
        hb[c, h * NX + x] = (gate / (1.0 + jnp.exp(-gate)) * acc[:, FFS:]).astype(jnp.bfloat16)
        mine = hb.at[c, h * NX + x]
        for d in (1, 3, 2):
            send(mine, mine, h_s.at[c, d], h_r.at[c, 4 - d], dev(dx=d))
        send(mine, mine, hs_s.at[c, 0], hs_r.at[c, 0], dev(sib=True))

    def h_forward(c):
        for d in (1, 3, 2):
            block = hb.at[c, h * NX + (x + d) % NX]
            arrived(block, h_s.at[c, d], h_r.at[c, d])
            send(block, block, hs_s.at[c, d], hs_r.at[c, d], dev(sib=True))

    def down(c):
        for d in (0, 1, 3, 2):
            block = hb.at[c, (1 - h) * NX + (x + d) % NX]
            arrived(block, hs_s.at[c, d], hs_r.at[c, d])
        for start, width in ((0, 512), (512, 384)):
            total = jnp.zeros((256, width), jnp.float32)
            for b in range(8):
                total = total + jnp.dot(
                    hb[c, b],
                    wd[b * FFS : (b + 1) * FFS, start : start + width],
                    preferred_element_type=jnp.float32,
                )
            dacc[:, start : start + width] = total
        for yr in range(NY):
            for j in range(4):
                rows = jnp.concatenate(
                    [
                        dacc[yr * 64 + xs * 16 + j * 4 : yr * 64 + xs * 16 + j * 4 + 4, :]
                        for xs in range(NX)
                    ],
                    axis=0,
                ).astype(jnp.bfloat16)
                slot = 4 * c + j
                if yr == 0 and slot == 0:
                    rb[req] = rows
                else:
                    obs[c, yr, j] = rows
                    send(
                        obs.at[c, yr, j],
                        rb.at[req],
                        r_s.at[yr, slot],
                        r_r.at[yr, slot],
                        dev(dy=YREL[yr], dz=ZREL[slot]),
                    )

    select(0)
    y_wait(0, 1)
    x_send(0, 1)
    y_wait(0, 2)
    x_send(0, 2)
    y_wait(0, 3)
    x_send(0, 3)
    x_forward(0, 0)
    select(1)
    x_forward(0, 1)
    y_wait(1, 1)
    x_send(1, 1)
    y_wait(1, 2)
    x_send(1, 2)
    x_forward(0, 2)
    y_wait(1, 3)
    x_send(1, 3)
    x_forward(0, 3)
    for yr in range(NY):
        x_far(0, yr)
    for load in loads:
        load.wait()
    x_forward(1, 0)
    sib_wait(0)
    up(0)
    x_forward(1, 1)
    x_forward(1, 2)
    x_forward(1, 3)
    h_forward(0)
    down(0)
    for yr in range(NY):
        x_far(1, yr)
    sib_wait(1)
    up(1)

    for d in (1, 3, 2):
        arrived(xi.at[(x + d) % NX], xi_s.at[d], xi_r.at[d])
    weights = xi[...].reshape(NX * TOK, 128)
    high = weights.astype(jnp.bfloat16)
    low = (weights - high.astype(jnp.float32)).astype(jnp.bfloat16)
    q = lax.broadcasted_iota(jnp.int32, (128, 512), 0)
    m = lax.broadcasted_iota(jnp.int32, (128, 512), 1)
    spread = (q == (m // 16) * CAP + m % CAP).astype(jnp.bfloat16)
    tr = lax.broadcasted_iota(jnp.int32, (32, 512), 0)
    tc = lax.broadcasted_iota(jnp.int32, (32, 512), 1)
    keep = tr // TOK == (tc // CAP) % NX
    wide = [
        jnp.where(keep, jnp.dot(part, spread, preferred_element_type=jnp.float32), 0.0).astype(jnp.bfloat16)
        for part in (high, low)
    ]

    h_forward(1)
    down(1)
    for yr in range(NY):
        for slot in range(NZ):
            if yr or slot:
                source = ((y - YREL[yr]) % NY) * NZ + (z - ZREL[slot]) % NZ
                arrived(rb.at[source], r_s.at[yr, slot], r_r.at[yr, slot])
    back = rb[...].reshape(512, OUTS)
    mixed = jnp.dot(wide[0], back, preferred_element_type=jnp.float32)
    mixed = mixed + jnp.dot(wide[1], back, preferred_element_type=jnp.float32)
    fs[...] = mixed.reshape(NX, TOK, OUTS)
    fb[x] = fs[x]
    for d in (1, 3, 2):
        send(fs.at[(x + d) % NX], fb.at[x], f_s.at[d], f_r.at[4 - d], dev(dx=d))
    for d in (1, 3, 2):
        arrived(fb.at[(x + d) % NX], f_s.at[d], f_r.at[d])
    for g in range(NX):
        cols = slice(g * OUTS, (g + 1) * OUTS)
        out_ref[:, cols] = (hid[:, cols] + fb[g]).astype(jnp.bfloat16)
    for copy in sends:
        copy.wait_send()


def on_device(residual, attn_part, norm_gain, routes, gates, gate_weight, up_weight, down_weight):
    bf16, f32 = jnp.bfloat16, jnp.float32
    dma = pltpu.SemaphoreType.DMA
    vmem = pl.BlockSpec(memory_space=pltpu.VMEM)
    hbm = pl.BlockSpec(memory_space=pl.ANY)
    return pl.pallas_call(
        kernel,
        out_shape=jax.ShapeDtypeStruct((TOK, HALF), bf16),
        in_specs=[vmem] * 5 + [hbm] * 3,
        out_specs=vmem,
        scratch_shapes=[
            pltpu.VMEM((D, FFS), bf16),
            pltpu.VMEM((D, FFS), bf16),
            pltpu.VMEM((8 * FFS, OUTS), bf16),
            pltpu.VMEM((2, 16, HALF + QUART), bf16),
            pltpu.VMEM((TOK, HALF), f32),
            pltpu.VMEM((NZ, 16, QUART), bf16),
            pltpu.VMEM((NZ, TOK, 128), f32),
            pltpu.VMEM((NX, TOK, 128), f32),
            pltpu.VMEM((2, NY, 16, HALF), bf16),
            pltpu.VMEM((2, 2, NY, NX, 16, HALF), bf16),
            pltpu.VMEM((256, 2 * FFS), f32),
            pltpu.VMEM((2, 8, 256, FFS), bf16),
            pltpu.VMEM((256, OUTS), f32),
            pltpu.VMEM((2, NY, 4, 16, OUTS), bf16),
            pltpu.VMEM((32, 16, OUTS), bf16),
            pltpu.VMEM((NX, TOK, OUTS), f32),
            pltpu.VMEM((NX, TOK, OUTS), f32),
            dma((3,)),
            dma((1,)),
            dma((1,)),
            dma((NZ,)),
            dma((NZ,)),
            dma((NZ,)),
            dma((NZ,)),
            dma((NX,)),
            dma((NX,)),
            dma((2, NY)),
            dma((2, NY)),
            dma((2, NY, 2)),
            dma((2, NY, 2)),
            dma((2, NY, 2)),
            dma((2, NY, 2)),
            dma((2, NY, 4)),
            dma((2, NY, 4)),
            dma((2, NX)),
            dma((2, NX)),
            dma((2, NX)),
            dma((2, NX)),
            dma((NY, NZ)),
            dma((NY, NZ)),
            dma((NX,)),
            dma((NX,)),
        ],
        compiler_params=pltpu.CompilerParams(
            collective_id=0, has_side_effects=True, vmem_limit_bytes=48 * 2**20
        ),
    )(
        residual,
        attn_part.reshape(TOK, D),
        norm_gain.reshape(1, HALF),
        routes,
        gates,
        gate_weight,
        up_weight,
        down_weight,
    )


def solution(mesh):
    placed = (
        P(("req", "grp"), "head"),
        P("head", ("req", "grp"), None),
        P("head"),
        P(("req", "grp"), None),
        P(("req", "grp"), None),
        P("req", None, ("head", "grp")),
        P("req", None, ("head", "grp")),
        P("req", None, ("head", "grp")),
    )
    return jax.shard_map(
        on_device, mesh=mesh, in_specs=placed, out_specs=P(("req", "grp"), "head"), check_vma=False
    )
```

```python
import functools

import jax
import jax.numpy as jnp
from jax import lax
from jax.experimental import pallas as pl
from jax.experimental.pallas import tpu as pltpu
from jax.sharding import PartitionSpec as P

MESH = pl.DeviceIdType.MESH
D = 7168
HALF = D // 2
QUART = HALF // 2
CAP = 4
TOK = 8
NX, NY, NZ = 4, 4, 8
ROWS = 128
ZBAR = (1, 2, 4, 6, 7)
CA = 2560
CB = HALF - CA
UA, UB = CA // 2, CB // 2
FFS = 256
OUTS = 896
EPSILON = 1e-06

ZREL = (0, 2, 6, 4, 1, 7, 3, 5)
YREL = (0, 1, 3, 2)
ZSLOT = {rel: slot for slot, rel in enumerate(ZREL)}
YSLOT = {rel: slot for slot, rel in enumerate(YREL)}


def kernel(
    res_hbm,
    attn_hbm,
    gain_hbm,
    routes_hbm,
    gates_hbm,
    wg_hbm,
    wu_hbm,
    wd_hbm,
    out_ref,
    res_ref,
    attn_ref,
    gain_ref,
    routes_ref,
    gates_ref,
    wg,
    wu,
    wd,
    ex,
    hid,
    za,
    zb,
    xi,
    ysel,
    ybel,
    xb,
    acc,
    hb,
    dacc,
    obs,
    rb,
    fs,
    fb,
    isem,
    wsem,
    ex_s,
    ex_r,
    za_s,
    za_r,
    zb_s,
    zb_r,
    xb_s,
    xb_r,
    xi_s,
    xi_r,
    y_s,
    y_r,
    yb_s,
    yb_r,
    xn_s,
    xn_r,
    xf_s,
    xf_r,
    sib_s,
    sib_r,
    h_s,
    h_r,
    hs_s,
    hs_r,
    r_s,
    r_r,
    f_s,
    f_r,
):
    req, h, x = lax.axis_index("req"), lax.axis_index("head"), lax.axis_index("grp")
    y, z = req // NZ, req % NZ

    def dev(dx=0, dy=0, dz=0, sib=False):
        return {
            "req": ((y + dy) % NY) * NZ + (z + dz) % NZ,
            "head": 1 - h if sib else h,
            "grp": (x + dx) % NX,
        }

    sends = []

    def send(src, dst, ssem, rsem, to):
        copy = pltpu.make_async_remote_copy(
            src_ref=src, dst_ref=dst, send_sem=ssem, recv_sem=rsem, device_id=to, device_id_type=MESH
        )
        copy.start()
        sends.append(copy)

    def arrived(dst, ssem, rsem):
        pltpu.make_async_remote_copy(
            src_ref=dst, dst_ref=dst, send_sem=ssem, recv_sem=rsem, device_id=dev(sib=True), device_id_type=MESH
        ).wait_recv()

    pairs = (
        (attn_hbm.at[0], attn_ref),
        (res_hbm, res_ref),
        (routes_hbm, routes_ref),
        (gates_hbm, gates_ref),
        (gain_hbm, gain_ref),
    )
    inputs = [pltpu.make_async_copy(src, dst, isem.at[i]) for i, (src, dst) in enumerate(pairs)]
    for copy in inputs:
        copy.start()
    loads = [
        pltpu.make_async_copy(src.at[0], dst, wsem.at[i])
        for i, (src, dst) in enumerate(((wg_hbm, wg), (wu_hbm, wu), (wd_hbm, wd)))
    ]

    bar = pltpu.get_barrier_semaphore()
    peers = [dev(sib=True)] + [dev(dx=d) for d in range(1, NX)]
    peers += [dev(dy=d) for d in range(1, NY)] + [dev(dz=d) for d in ZBAR]
    for peer in peers:
        pl.semaphore_signal(bar, inc=1, device_id=peer, device_id_type=MESH)

    for copy in inputs:
        copy.wait()
    attn = attn_ref[...].astype(jnp.float32)
    res = res_ref[...].astype(jnp.float32)
    ex[0, :, :HALF] = jnp.concatenate([attn[:, :HALF], attn[:, HALF:]], axis=0).astype(jnp.bfloat16)
    ex[0, :, HALF:] = jnp.concatenate([res[:, :QUART], res[:, QUART:]], axis=0).astype(jnp.bfloat16)

    routes = routes_ref[...]
    gates = gates_ref[...]
    column = lax.broadcasted_iota(jnp.int32, (TOK, 128), 1)
    named = jnp.zeros((TOK, 128), jnp.float32)
    value = jnp.zeros((TOK, 128), jnp.float32)
    for k in range(8):
        hit = (routes[:, k : k + 1] == column // CAP).astype(jnp.float32)
        named = named + hit
        value = value + hit * gates[:, k : k + 1]
    row = lax.broadcasted_iota(jnp.int32, (TOK, 128), 0)
    before = jnp.zeros((TOK, 128), jnp.float32)
    for t in range(TOK - 1):
        before = before + jnp.where(row > t, named[t : t + 1, :], 0.0)
    info = jnp.where(before == (column % CAP).astype(jnp.float32), value, 0.0)
    xi[x] = info
    table = jnp.concatenate([info, info], axis=0)
    table = (table != 0.0).astype(jnp.float32).astype(jnp.bfloat16)
    za[0, :, UA:] = table
    zb[0, x, :, UB:] = table

    pl.semaphore_wait(bar, len(peers))
    send(ex.at[0], ex.at[1], ex_s.at[0], ex_r.at[0], dev(sib=True))
    for d in (1, 3, 2):
        send(xi.at[x], xi.at[x], xi_s.at[d], xi_r.at[4 - d], dev(dx=d))

    arrived(ex.at[1], ex_s.at[0], ex_r.at[0])
    theirs = ex[1].astype(jnp.float32)
    t_attn = (theirs[:TOK, :HALF], theirs[TOK:, :HALF])
    m_attn = (attn[:, :HALF], attn[:, HALF:])
    t_res = jnp.concatenate([theirs[:TOK, HALF:], theirs[TOK:, HALF:]], axis=1)
    sums = (m_attn[0] + t_attn[0], m_attn[1] + t_attn[1])
    first = h == 0
    own = res + jnp.where(first, sums[0], sums[1])
    other = t_res + jnp.where(first, sums[1], sums[0])
    squares = jnp.sum(own * own, axis=1, keepdims=True) + jnp.sum(other * other, axis=1, keepdims=True)
    scale = lax.rsqrt(squares / D + EPSILON)
    gain = jnp.concatenate([gain_ref[i : i + 1, :] for i in range(HALF // 128)], axis=1)
    normed = own * scale * gain
    hid[...] = own
    a_cols, b_cols = normed[:, :CA], normed[:, CA:]
    za[0, :, :UA] = jnp.concatenate([a_cols[:, :UA], a_cols[:, UA:]], axis=0).astype(jnp.bfloat16)
    zb[0, x, :, :UB] = jnp.concatenate([b_cols[:, :UB], b_cols[:, UB:]], axis=0).astype(jnp.bfloat16)

    def z_send(buf, ssem, rsem, d):
        slot = ZSLOT[(-d) % NZ]
        send(buf.at[0], buf.at[slot], ssem.at[slot], rsem.at[slot], dev(dz=d))

    def z_wait(buf, ssem, rsem, rel):
        slot = ZSLOT[rel]
        arrived(buf.at[slot], ssem.at[slot], rsem.at[slot])

    def z_relay(buf, ssem, rsem, rel):
        third, onward = (3, 7) if rel == 2 else (5, 1)
        slot = ZSLOT[third]
        send(buf.at[ZSLOT[rel]], buf.at[slot], ssem.at[slot], rsem.at[slot], dev(dz=onward))

    def z_first(buf, ssem, rsem):
        for rel in (2, 6):
            z_wait(buf, ssem, rsem, rel)
            z_relay(buf, ssem, rsem, rel)
        for d in (7, 1):
            z_send(buf, ssem, rsem, d)
        z_wait(buf, ssem, rsem, 4)

    def z_second(buf, ssem, rsem):
        for rel in (1, 7, 3, 5):
            z_wait(buf, ssem, rsem, rel)

    for d in (6, 2, 4):
        z_send(za, za_s, za_r, d)
    for d in (1, 3, 2):
        send(zb.at[0, x], zb.at[0, x], xb_s.at[d], xb_r.at[4 - d], dev(dx=d))

    left, right = (x + 3) % NX, (x + 1) % NX

    def x_send(c, yr):
        piece = xb.at[c, h, yr, x, :, pl.ds(0, CA)]
        send(piece, piece, xn_s.at[c, yr, 0], xn_r.at[c, yr, 0], dev(dx=1))
        send(piece, piece, xn_s.at[c, yr, 1], xn_r.at[c, yr, 1], dev(dx=3))
        send(piece, piece, sib_s.at[c, yr, 0], sib_r.at[c, yr, 0], dev(sib=True))

    def x_forward(c, yr):
        for way, source, to in ((0, left, 1), (1, right, 3)):
            piece = xb.at[c, h, yr, source, :, pl.ds(0, CA)]
            arrived(piece, xn_s.at[c, yr, way], xn_r.at[c, yr, way])
            part = xb.at[c, h, yr, source, :, pl.ds(way * UA, UA)]
            send(part, part, xf_s.at[c, yr, way], xf_r.at[c, yr, way], dev(dx=to))
            send(piece, piece, sib_s.at[c, yr, 1 + way], sib_r.at[c, yr, 1 + way], dev(sib=True))

    def x_far(c, yr):
        far = (x + 2) % NX
        for way in (0, 1):
            part = xb.at[c, h, yr, far, :, pl.ds(way * UA, UA)]
            arrived(part, xf_s.at[c, yr, way], xf_r.at[c, yr, way])
        piece = xb.at[c, h, yr, far, :, pl.ds(0, CA)]
        send(piece, piece, sib_s.at[c, yr, 3], sib_r.at[c, yr, 3], dev(sib=True))

    def sib_wait(k):
        c = k // 2
        for yr in (k % 2 * 2, k % 2 * 2 + 1):
            for kind, source in enumerate((x, left, right, (x + 2) % NX)):
                piece = xb.at[c, 1 - h, yr, source, :, pl.ds(0, CA)]
                arrived(piece, sib_s.at[c, yr, kind], sib_r.at[c, yr, kind])
            arrived(b_rows(c, 1 - h, yr), sib_s.at[c, yr, 4], sib_r.at[c, yr, 4])

    def y_wait(c, yr):
        piece = xb.at[c, h, yr, x, :, pl.ds(0, CA)]
        arrived(piece, y_s.at[c, yr], y_r.at[c, yr])

    def b_rows(c, half_index, yr):
        return xb.at[c, half_index, yr, :, :, pl.ds(CA, CB)]

    def b_sib(c, yr):
        piece = b_rows(c, h, yr)
        send(piece, piece, sib_s.at[c, yr, 4], sib_r.at[c, yr, 4], dev(sib=True))

    def b_wait(c, yr):
        arrived(b_rows(c, h, yr), yb_s.at[c, yr], yb_r.at[c, yr])
        b_sib(c, yr)

    def choose(tables, blocks):
        table = jnp.concatenate(tables, axis=0)
        rows16 = lax.broadcasted_iota(jnp.int32, (16, 128), 0) % CAP
        cols16 = lax.broadcasted_iota(jnp.int32, (16, 128), 1)
        pick = jnp.concatenate(
            [
                (cols16 == rows16 + (((y + rel) % NY) * NZ + z) * CAP).astype(jnp.float32)
                for rel in YREL
            ],
            axis=0,
        ).astype(jnp.bfloat16)
        small = lax.dot_general(
            pick, table, (((1,), (1,)), ((), ())), preferred_element_type=jnp.float32
        )
        r = lax.broadcasted_iota(jnp.int32, (64, 64), 0)
        m = lax.broadcasted_iota(jnp.int32, (64, 64), 1)
        chosen = []
        for u in (0, 1):
            mask = ((r // 4) % 4 == m // 16) & ((m // 8) % 2 == u)
            onehot = jnp.where(mask, small, 0.0).astype(jnp.bfloat16)
            chosen.append(jnp.dot(onehot, blocks, preferred_element_type=jnp.float32).astype(jnp.bfloat16))
        return chosen

    def select_a(c):
        group = range(4 * c, 4 * c + 4)
        chosen = choose([za[slot, :, UA:] for slot in group], za[4 * c : 4 * c + 4, :, :UA].reshape(64, UA))
        for u in (0, 1):
            xb[c, h, 0, x, :, u * UA : (u + 1) * UA] = chosen[u][:16]
            for yr in range(1, NY):
                ysel[c, yr, :, u * UA : (u + 1) * UA] = chosen[u][16 * yr : 16 * yr + 16]
        for yr in (1, 2, 3):
            back = YSLOT[(-YREL[yr]) % NY]
            send(
                ysel.at[c, yr],
                xb.at[c, h, back, x, :, pl.ds(0, CA)],
                y_s.at[c, back],
                y_r.at[c, back],
                dev(dy=YREL[yr]),
            )

    def select_b(c):
        group = range(4 * c, 4 * c + 4)
        for xs in range(NX):
            chosen = choose(
                [zb[slot, xs, :, UB:] for slot in group], zb[4 * c : 4 * c + 4, xs, :, :UB].reshape(64, UB)
            )
            for u in (0, 1):
                xb[c, h, 0, xs, :, CA + u * UB : CA + (u + 1) * UB] = chosen[u][:16]
                for yr in range(1, NY):
                    ybel[c, yr, xs, :, u * UB : (u + 1) * UB] = chosen[u][16 * yr : 16 * yr + 16]
        for yr in (1, 2, 3):
            back = YSLOT[(-YREL[yr]) % NY]
            send(ybel.at[c, yr], b_rows(c, h, back), yb_s.at[c, back], yb_r.at[c, back], dev(dy=YREL[yr]))
        b_sib(c, 0)

    def up(k):
        c, yp = k // 2, k % 2 * 2
        acc[...] = jnp.zeros_like(acc)

        def step(i, carry):
            part = xb[c, i // 2, yp : yp + 2, :, :, pl.ds(pl.multiple_of((i % 2) * QUART, QUART), QUART)]
            rows = part.reshape(ROWS, QUART)
            ks = pl.ds(pl.multiple_of(i * QUART, QUART), QUART)
            acc[:, :FFS] += jnp.dot(rows, wg[ks, :], preferred_element_type=jnp.float32)
            acc[:, FFS:] += jnp.dot(rows, wu[ks, :], preferred_element_type=jnp.float32)
            return carry

        lax.fori_loop(0, 4, step, 0)
        gate = acc[:, :FFS]
        hb[k, h * NX + x] = (gate / (1.0 + jnp.exp(-gate)) * acc[:, FFS:]).astype(jnp.bfloat16)
        mine = hb.at[k, h * NX + x]
        for d in (1, 3, 2):
            send(mine, mine, h_s.at[k, d], h_r.at[k, 4 - d], dev(dx=d))
        send(mine, mine, hs_s.at[k, 0], hs_r.at[k, 0], dev(sib=True))

    def h_forward(k):
        for d in (1, 3, 2):
            block = hb.at[k, h * NX + (x + d) % NX]
            arrived(block, h_s.at[k, d], h_r.at[k, d])
            send(block, block, hs_s.at[k, d], hs_r.at[k, d], dev(sib=True))

    def down(k):
        c, yp = k // 2, k % 2 * 2
        for d in (0, 1, 3, 2):
            block = hb.at[k, (1 - h) * NX + (x + d) % NX]
            arrived(block, hs_s.at[k, d], hs_r.at[k, d])
        for start, width in ((0, 512), (512, 384)):
            total = jnp.zeros((ROWS, width), jnp.float32)
            for b in range(8):
                total = total + jnp.dot(
                    hb[k, b],
                    wd[b * FFS : (b + 1) * FFS, start : start + width],
                    preferred_element_type=jnp.float32,
                )
            dacc[:, start : start + width] = total
        for yi in range(2):
            for j in range(4):
                yr, slot = yp + yi, 4 * c + j
                rows = jnp.concatenate(
                    [
                        dacc[yi * 64 + xs * 16 + j * 4 : yi * 64 + xs * 16 + j * 4 + 4, :]
                        for xs in range(NX)
                    ],
                    axis=0,
                ).astype(jnp.bfloat16)
                if yr == 0 and slot == 0:
                    rb[req] = rows
                else:
                    obs[c, yr, j] = rows
                    send(
                        obs.at[c, yr, j],
                        rb.at[req],
                        r_s.at[yr, slot],
                        r_r.at[yr, slot],
                        dev(dy=YREL[yr], dz=ZREL[slot]),
                    )

    for d in (1, 3, 2):
        arrived(zb.at[0, (x + d) % NX], xb_s.at[d], xb_r.at[d])
    for d in (6, 2, 4):
        z_send(zb, zb_s, zb_r, d)
    for load in loads:
        load.start()
    z_first(za, za_s, za_r)
    select_a(0)
    x_send(0, 0)
    for yr in (1, 2, 3):
        y_wait(0, yr)
        x_send(0, yr)
    z_first(zb, zb_s, zb_r)
    x_forward(0, 0)
    select_b(0)
    z_second(za, za_s, za_r)
    select_a(1)
    x_send(1, 0)
    x_forward(0, 1)
    x_forward(0, 2)
    x_forward(0, 3)
    for yr in (1, 2, 3):
        y_wait(1, yr)
        x_send(1, yr)
    b_wait(0, 1)
    b_wait(0, 2)
    b_wait(0, 3)
    z_second(zb, zb_s, zb_r)
    select_b(1)
    for load in loads:
        load.wait()
    x_far(0, 0)
    x_far(0, 1)
    sib_wait(0)
    up(0)
    x_far(0, 2)
    x_far(0, 3)
    sib_wait(1)
    up(1)
    x_forward(1, 0)
    x_forward(1, 1)
    x_forward(1, 2)
    h_forward(0)
    down(0)
    x_forward(1, 3)
    h_forward(1)
    down(1)
    b_wait(1, 1)
    b_wait(1, 2)
    b_wait(1, 3)
    x_far(1, 0)
    x_far(1, 1)
    sib_wait(2)
    up(2)
    x_far(1, 2)
    x_far(1, 3)
    sib_wait(3)
    up(3)

    for d in (1, 3, 2):
        arrived(xi.at[(x + d) % NX], xi_s.at[d], xi_r.at[d])
    weights = xi[...].reshape(NX * TOK, 128)
    high = weights.astype(jnp.bfloat16)
    low = (weights - high.astype(jnp.float32)).astype(jnp.bfloat16)
    q = lax.broadcasted_iota(jnp.int32, (128, 512), 0)
    m = lax.broadcasted_iota(jnp.int32, (128, 512), 1)
    spread = (q == (m // 16) * CAP + m % CAP).astype(jnp.bfloat16)
    tr = lax.broadcasted_iota(jnp.int32, (32, 512), 0)
    tc = lax.broadcasted_iota(jnp.int32, (32, 512), 1)
    keep = tr // TOK == (tc // CAP) % NX
    wide = [
        jnp.where(keep, jnp.dot(part, spread, preferred_element_type=jnp.float32), 0.0).astype(jnp.bfloat16)
        for part in (high, low)
    ]

    h_forward(2)
    down(2)
    h_forward(3)
    down(3)
    for yr in range(NY):
        for slot in range(NZ):
            if yr or slot:
                source = ((y - YREL[yr]) % NY) * NZ + (z - ZREL[slot]) % NZ
                arrived(rb.at[source], r_s.at[yr, slot], r_r.at[yr, slot])
    back = rb[...].reshape(512, OUTS)
    mixed = jnp.dot(wide[0], back, preferred_element_type=jnp.float32)
    mixed = mixed + jnp.dot(wide[1], back, preferred_element_type=jnp.float32)
    fs[...] = mixed.reshape(NX, TOK, OUTS)
    fb[x] = fs[x]
    for d in (1, 3, 2):
        send(fs.at[(x + d) % NX], fb.at[x], f_s.at[d], f_r.at[4 - d], dev(dx=d))
    for d in (1, 3, 2):
        arrived(fb.at[(x + d) % NX], f_s.at[d], f_r.at[d])
    for g in range(NX):
        cols = slice(g * OUTS, (g + 1) * OUTS)
        out_ref[:, cols] = (hid[:, cols] + fb[g]).astype(jnp.bfloat16)
    for copy in sends:
        copy.wait_send()


def on_device(residual, attn_part, norm_gain, routes, gates, gate_weight, up_weight, down_weight):
    bf16, f32 = jnp.bfloat16, jnp.float32
    dma = pltpu.SemaphoreType.DMA
    vmem = pl.BlockSpec(memory_space=pltpu.VMEM)
    hbm = pl.BlockSpec(memory_space=pl.ANY)
    return pl.pallas_call(
        kernel,
        out_shape=jax.ShapeDtypeStruct((TOK, HALF), bf16),
        in_specs=[hbm] * 8,
        out_specs=vmem,
        scratch_shapes=[
            pltpu.VMEM((TOK, HALF), bf16),
            pltpu.VMEM((TOK, D), bf16),
            pltpu.VMEM((HALF // 128, 128), f32),
            pltpu.VMEM((TOK, TOK), jnp.int32),
            pltpu.VMEM((TOK, TOK), f32),
            pltpu.VMEM((D, FFS), bf16),
            pltpu.VMEM((D, FFS), bf16),
            pltpu.VMEM((8 * FFS, OUTS), bf16),
            pltpu.VMEM((2, 16, HALF + QUART), bf16),
            pltpu.VMEM((TOK, HALF), f32),
            pltpu.VMEM((NZ, 16, UA + 128), bf16),
            pltpu.VMEM((NZ, NX, 16, UB + 128), bf16),
            pltpu.VMEM((NX, TOK, 128), f32),
            pltpu.VMEM((2, NY, 16, CA), bf16),
            pltpu.VMEM((2, NY, NX, 16, CB), bf16),
            pltpu.VMEM((2, 2, NY, NX, 16, HALF), bf16),
            pltpu.VMEM((ROWS, 2 * FFS), f32),
            pltpu.VMEM((4, 8, ROWS, FFS), bf16),
            pltpu.VMEM((ROWS, OUTS), f32),
            pltpu.VMEM((2, NY, 4, 16, OUTS), bf16),
            pltpu.VMEM((32, 16, OUTS), bf16),
            pltpu.VMEM((NX, TOK, OUTS), f32),
            pltpu.VMEM((NX, TOK, OUTS), f32),
            dma((5,)),
            dma((3,)),
            dma((1,)),
            dma((1,)),
            dma((NZ,)),
            dma((NZ,)),
            dma((NZ,)),
            dma((NZ,)),
            dma((NX,)),
            dma((NX,)),
            dma((NX,)),
            dma((NX,)),
            dma((2, NY)),
            dma((2, NY)),
            dma((2, NY)),
            dma((2, NY)),
            dma((2, NY, 2)),
            dma((2, NY, 2)),
            dma((2, NY, 2)),
            dma((2, NY, 2)),
            dma((2, NY, 5)),
            dma((2, NY, 5)),
            dma((4, NX)),
            dma((4, NX)),
            dma((4, NX)),
            dma((4, NX)),
            dma((NY, NZ)),
            dma((NY, NZ)),
            dma((NX,)),
            dma((NX,)),
        ],
        compiler_params=pltpu.CompilerParams(
            collective_id=0, has_side_effects=True, vmem_limit_bytes=60 * 2**20
        ),
    )(
        residual,
        attn_part,
        norm_gain.reshape(HALF // 128, 128),
        routes,
        gates,
        gate_weight,
        up_weight,
        down_weight,
    )


def solution(mesh):
    placed = (
        P(("req", "grp"), "head"),
        P("head", ("req", "grp"), None),
        P("head"),
        P(("req", "grp"), None),
        P(("req", "grp"), None),
        P("req", None, ("head", "grp")),
        P("req", None, ("head", "grp")),
        P("req", None, ("head", "grp")),
    )
    return jax.shard_map(
        on_device, mesh=mesh, in_specs=placed, out_specs=P(("req", "grp"), "head"), check_vma=False
    )
```

```python
import functools

import jax
import jax.numpy as jnp
from jax import lax
from jax.experimental import pallas as pl
from jax.experimental.pallas import tpu as pltpu
from jax.sharding import PartitionSpec as P

MESH = pl.DeviceIdType.MESH
D = 7168
HALF = D // 2
QUART = HALF // 2
CAP = 4
TOK = 8
NX, NY, NZ = 4, 4, 8
ROWS = 128
ZBAR = (1, 2, 3, 4, 5, 6, 7)
CA = 2560
CB = HALF - CA
UA, UB = CA // 2, CB // 2
FFS = 256
OUTS = 896
EPSILON = 1e-06

ZREL = (0, 4, 3, 5, 1, 7, 2, 6)
YREL = (0, 1, 3, 2)
ZSLOT = {rel: slot for slot, rel in enumerate(ZREL)}
YSLOT = {rel: slot for slot, rel in enumerate(YREL)}


def kernel(
    res_hbm,
    attn_hbm,
    gain_hbm,
    routes_hbm,
    gates_hbm,
    wg_hbm,
    wu_hbm,
    wd_hbm,
    out_ref,
    res_ref,
    attn_ref,
    gain_ref,
    routes_ref,
    gates_ref,
    wg,
    wu,
    wd,
    ex,
    hid,
    za,
    zb,
    xi,
    ysel,
    ybel,
    xb,
    acc,
    hb,
    dacc,
    obs,
    rb,
    fs,
    fb,
    isem,
    wsem,
    ex_s,
    ex_r,
    za_s,
    za_r,
    zb_s,
    zb_r,
    xb_s,
    xb_r,
    xi_s,
    xi_r,
    y_s,
    y_r,
    yb_s,
    yb_r,
    xn_s,
    xn_r,
    xf_s,
    xf_r,
    sib_s,
    sib_r,
    h_s,
    h_r,
    hs_s,
    hs_r,
    r_s,
    r_r,
    f_s,
    f_r,
):
    req, h, x = lax.axis_index("req"), lax.axis_index("head"), lax.axis_index("grp")
    y, z = req // NZ, req % NZ

    def dev(dx=0, dy=0, dz=0, sib=False):
        return {
            "req": ((y + dy) % NY) * NZ + (z + dz) % NZ,
            "head": 1 - h if sib else h,
            "grp": (x + dx) % NX,
        }

    sends = []

    def send(src, dst, ssem, rsem, to):
        copy = pltpu.make_async_remote_copy(
            src_ref=src, dst_ref=dst, send_sem=ssem, recv_sem=rsem, device_id=to, device_id_type=MESH
        )
        copy.start()
        sends.append(copy)

    def arrived(dst, ssem, rsem):
        pltpu.make_async_remote_copy(
            src_ref=dst, dst_ref=dst, send_sem=ssem, recv_sem=rsem, device_id=dev(sib=True), device_id_type=MESH
        ).wait_recv()

    pairs = (
        (attn_hbm.at[0], attn_ref),
        (res_hbm, res_ref),
        (routes_hbm, routes_ref),
        (gates_hbm, gates_ref),
        (gain_hbm, gain_ref),
    )
    inputs = [pltpu.make_async_copy(src, dst, isem.at[i]) for i, (src, dst) in enumerate(pairs)]
    for copy in inputs:
        copy.start()
    loads = [
        pltpu.make_async_copy(src.at[0], dst, wsem.at[i])
        for i, (src, dst) in enumerate(((wg_hbm, wg), (wu_hbm, wu), (wd_hbm, wd)))
    ]

    bar = pltpu.get_barrier_semaphore()
    peers = [dev(sib=True)] + [dev(dx=d) for d in range(1, NX)]
    peers += [dev(dy=d) for d in range(1, NY)] + [dev(dz=d) for d in ZBAR]
    for peer in peers:
        pl.semaphore_signal(bar, inc=1, device_id=peer, device_id_type=MESH)

    for copy in inputs:
        copy.wait()
    attn = attn_ref[...].astype(jnp.float32)
    res = res_ref[...].astype(jnp.float32)
    ex[0, :, :HALF] = jnp.concatenate([attn[:, :HALF], attn[:, HALF:]], axis=0).astype(jnp.bfloat16)
    ex[0, :, HALF:] = jnp.concatenate([res[:, :QUART], res[:, QUART:]], axis=0).astype(jnp.bfloat16)

    routes = routes_ref[...]
    gates = gates_ref[...]
    column = lax.broadcasted_iota(jnp.int32, (TOK, 128), 1)
    named = jnp.zeros((TOK, 128), jnp.float32)
    value = jnp.zeros((TOK, 128), jnp.float32)
    for k in range(8):
        hit = (routes[:, k : k + 1] == column // CAP).astype(jnp.float32)
        named = named + hit
        value = value + hit * gates[:, k : k + 1]
    row = lax.broadcasted_iota(jnp.int32, (TOK, 128), 0)
    before = jnp.zeros((TOK, 128), jnp.float32)
    for t in range(TOK - 1):
        before = before + jnp.where(row > t, named[t : t + 1, :], 0.0)
    info = jnp.where(before == (column % CAP).astype(jnp.float32), value, 0.0)
    xi[x] = info
    table = jnp.concatenate([info, info], axis=0)
    table = (table != 0.0).astype(jnp.float32).astype(jnp.bfloat16)
    za[0, :, UA:] = table
    zb[0, x, :, UB:] = table

    pl.semaphore_wait(bar, len(peers))
    send(ex.at[0], ex.at[1], ex_s.at[0], ex_r.at[0], dev(sib=True))
    for d in (1, 3, 2):
        send(xi.at[x], xi.at[x], xi_s.at[d], xi_r.at[4 - d], dev(dx=d))

    arrived(ex.at[1], ex_s.at[0], ex_r.at[0])
    theirs = ex[1].astype(jnp.float32)
    t_attn = (theirs[:TOK, :HALF], theirs[TOK:, :HALF])
    m_attn = (attn[:, :HALF], attn[:, HALF:])
    t_res = jnp.concatenate([theirs[:TOK, HALF:], theirs[TOK:, HALF:]], axis=1)
    sums = (m_attn[0] + t_attn[0], m_attn[1] + t_attn[1])
    first = h == 0
    own = res + jnp.where(first, sums[0], sums[1])
    other = t_res + jnp.where(first, sums[1], sums[0])
    squares = jnp.sum(own * own, axis=1, keepdims=True) + jnp.sum(other * other, axis=1, keepdims=True)
    scale = lax.rsqrt(squares / D + EPSILON)
    gain = jnp.concatenate([gain_ref[i : i + 1, :] for i in range(HALF // 128)], axis=1)
    normed = own * scale * gain
    hid[...] = own
    a_cols, b_cols = normed[:, :CA], normed[:, CA:]
    za[0, :, :UA] = jnp.concatenate([a_cols[:, :UA], a_cols[:, UA:]], axis=0).astype(jnp.bfloat16)
    zb[0, x, :, :UB] = jnp.concatenate([b_cols[:, :UB], b_cols[:, UB:]], axis=0).astype(jnp.bfloat16)

    def z_send(buf, ssem, rsem, d):
        slot = ZSLOT[(-d) % NZ]
        send(buf.at[0], buf.at[slot], ssem.at[slot], rsem.at[slot], dev(dz=d))

    def z_wait(buf, ssem, rsem, rel):
        slot = ZSLOT[rel]
        arrived(buf.at[slot], ssem.at[slot], rsem.at[slot])

    def z_first(buf, ssem, rsem):
        for rel in (3, 5, 4):
            z_wait(buf, ssem, rsem, rel)
        for d in (7, 1, 6, 2):
            z_send(buf, ssem, rsem, d)

    def z_second(buf, ssem, rsem):
        for rel in (1, 7, 2, 6):
            z_wait(buf, ssem, rsem, rel)

    for d in (5, 3, 4):
        z_send(za, za_s, za_r, d)
    for d in (1, 3, 2):
        send(zb.at[0, x], zb.at[0, x], xb_s.at[d], xb_r.at[4 - d], dev(dx=d))

    left, right = (x + 3) % NX, (x + 1) % NX

    def x_send(c, yr):
        piece = xb.at[c, h, yr, x, :, pl.ds(0, CA)]
        send(piece, piece, xn_s.at[c, yr, 0], xn_r.at[c, yr, 0], dev(dx=1))
        send(piece, piece, xn_s.at[c, yr, 1], xn_r.at[c, yr, 1], dev(dx=3))
        send(piece, piece, sib_s.at[c, yr, 0], sib_r.at[c, yr, 0], dev(sib=True))

    def x_forward(c, yr):
        for way, source, to in ((0, left, 1), (1, right, 3)):
            piece = xb.at[c, h, yr, source, :, pl.ds(0, CA)]
            arrived(piece, xn_s.at[c, yr, way], xn_r.at[c, yr, way])
            part = xb.at[c, h, yr, source, :, pl.ds(way * UA, UA)]
            send(part, part, xf_s.at[c, yr, way], xf_r.at[c, yr, way], dev(dx=to))
            send(piece, piece, sib_s.at[c, yr, 1 + way], sib_r.at[c, yr, 1 + way], dev(sib=True))

    def x_far(c, yr):
        far = (x + 2) % NX
        for way in (0, 1):
            part = xb.at[c, h, yr, far, :, pl.ds(way * UA, UA)]
            arrived(part, xf_s.at[c, yr, way], xf_r.at[c, yr, way])
        piece = xb.at[c, h, yr, far, :, pl.ds(0, CA)]
        send(piece, piece, sib_s.at[c, yr, 3], sib_r.at[c, yr, 3], dev(sib=True))

    def sib_wait(k):
        c = k // 2
        for yr in (k % 2 * 2, k % 2 * 2 + 1):
            for kind, source in enumerate((x, left, right, (x + 2) % NX)):
                piece = xb.at[c, 1 - h, yr, source, :, pl.ds(0, CA)]
                arrived(piece, sib_s.at[c, yr, kind], sib_r.at[c, yr, kind])
            arrived(b_rows(c, 1 - h, yr), sib_s.at[c, yr, 4], sib_r.at[c, yr, 4])

    def y_wait(c, yr):
        piece = xb.at[c, h, yr, x, :, pl.ds(0, CA)]
        arrived(piece, y_s.at[c, yr], y_r.at[c, yr])

    def b_rows(c, half_index, yr):
        return xb.at[c, half_index, yr, :, :, pl.ds(CA, CB)]

    def b_sib(c, yr):
        piece = b_rows(c, h, yr)
        send(piece, piece, sib_s.at[c, yr, 4], sib_r.at[c, yr, 4], dev(sib=True))

    def b_wait(c, yr):
        arrived(b_rows(c, h, yr), yb_s.at[c, yr], yb_r.at[c, yr])
        b_sib(c, yr)

    def choose(tables, blocks):
        table = jnp.concatenate(tables, axis=0)
        rows16 = lax.broadcasted_iota(jnp.int32, (16, 128), 0) % CAP
        cols16 = lax.broadcasted_iota(jnp.int32, (16, 128), 1)
        pick = jnp.concatenate(
            [
                (cols16 == rows16 + (((y + rel) % NY) * NZ + z) * CAP).astype(jnp.float32)
                for rel in YREL
            ],
            axis=0,
        ).astype(jnp.bfloat16)
        small = lax.dot_general(
            pick, table, (((1,), (1,)), ((), ())), preferred_element_type=jnp.float32
        )
        r = lax.broadcasted_iota(jnp.int32, (64, 64), 0)
        m = lax.broadcasted_iota(jnp.int32, (64, 64), 1)
        chosen = []
        for u in (0, 1):
            mask = ((r // 4) % 4 == m // 16) & ((m // 8) % 2 == u)
            onehot = jnp.where(mask, small, 0.0).astype(jnp.bfloat16)
            chosen.append(jnp.dot(onehot, blocks, preferred_element_type=jnp.float32).astype(jnp.bfloat16))
        return chosen

    def select_a(c):
        group = range(4 * c, 4 * c + 4)
        chosen = choose([za[slot, :, UA:] for slot in group], za[4 * c : 4 * c + 4, :, :UA].reshape(64, UA))
        for u in (0, 1):
            xb[c, h, 0, x, :, u * UA : (u + 1) * UA] = chosen[u][:16]
            for yr in range(1, NY):
                ysel[c, yr, :, u * UA : (u + 1) * UA] = chosen[u][16 * yr : 16 * yr + 16]
        for yr in (1, 2, 3):
            back = YSLOT[(-YREL[yr]) % NY]
            send(
                ysel.at[c, yr],
                xb.at[c, h, back, x, :, pl.ds(0, CA)],
                y_s.at[c, back],
                y_r.at[c, back],
                dev(dy=YREL[yr]),
            )

    def select_b(c):
        group = range(4 * c, 4 * c + 4)
        for xs in range(NX):
            chosen = choose(
                [zb[slot, xs, :, UB:] for slot in group], zb[4 * c : 4 * c + 4, xs, :, :UB].reshape(64, UB)
            )
            for u in (0, 1):
                xb[c, h, 0, xs, :, CA + u * UB : CA + (u + 1) * UB] = chosen[u][:16]
                for yr in range(1, NY):
                    ybel[c, yr, xs, :, u * UB : (u + 1) * UB] = chosen[u][16 * yr : 16 * yr + 16]
        for yr in (1, 2, 3):
            back = YSLOT[(-YREL[yr]) % NY]
            send(ybel.at[c, yr], b_rows(c, h, back), yb_s.at[c, back], yb_r.at[c, back], dev(dy=YREL[yr]))
        b_sib(c, 0)

    def up(k):
        c, yp = k // 2, k % 2 * 2
        acc[...] = jnp.zeros_like(acc)

        def step(i, carry):
            part = xb[c, i // 2, yp : yp + 2, :, :, pl.ds(pl.multiple_of((i % 2) * QUART, QUART), QUART)]
            rows = part.reshape(ROWS, QUART)
            ks = pl.ds(pl.multiple_of(i * QUART, QUART), QUART)
            acc[:, :FFS] += jnp.dot(rows, wg[ks, :], preferred_element_type=jnp.float32)
            acc[:, FFS:] += jnp.dot(rows, wu[ks, :], preferred_element_type=jnp.float32)
            return carry

        lax.fori_loop(0, 4, step, 0)
        gate = acc[:, :FFS]
        hb[k, h * NX + x] = (gate / (1.0 + jnp.exp(-gate)) * acc[:, FFS:]).astype(jnp.bfloat16)
        mine = hb.at[k, h * NX + x]
        for d in (1, 3, 2):
            send(mine, mine, h_s.at[k, d], h_r.at[k, 4 - d], dev(dx=d))
        send(mine, mine, hs_s.at[k, 0], hs_r.at[k, 0], dev(sib=True))

    def h_forward(k):
        for d in (1, 3, 2):
            block = hb.at[k, h * NX + (x + d) % NX]
            arrived(block, h_s.at[k, d], h_r.at[k, d])
            send(block, block, hs_s.at[k, d], hs_r.at[k, d], dev(sib=True))

    def down(k):
        c, yp = k // 2, k % 2 * 2
        for d in (0, 1, 3, 2):
            block = hb.at[k, (1 - h) * NX + (x + d) % NX]
            arrived(block, hs_s.at[k, d], hs_r.at[k, d])
        for start, width in ((0, 512), (512, 384)):
            total = jnp.zeros((ROWS, width), jnp.float32)
            for b in range(8):
                total = total + jnp.dot(
                    hb[k, b],
                    wd[b * FFS : (b + 1) * FFS, start : start + width],
                    preferred_element_type=jnp.float32,
                )
            dacc[:, start : start + width] = total
        for yi in range(2):
            for j in range(4):
                yr, slot = yp + yi, 4 * c + j
                rows = jnp.concatenate(
                    [
                        dacc[yi * 64 + xs * 16 + j * 4 : yi * 64 + xs * 16 + j * 4 + 4, :]
                        for xs in range(NX)
                    ],
                    axis=0,
                ).astype(jnp.bfloat16)
                if yr == 0 and slot == 0:
                    rb[req] = rows
                else:
                    obs[c, yr, j] = rows
                    send(
                        obs.at[c, yr, j],
                        rb.at[req],
                        r_s.at[yr, slot],
                        r_r.at[yr, slot],
                        dev(dy=YREL[yr], dz=ZREL[slot]),
                    )

    for d in (1, 3, 2):
        arrived(zb.at[0, (x + d) % NX], xb_s.at[d], xb_r.at[d])
    for d in (5, 3, 4):
        z_send(zb, zb_s, zb_r, d)
    for load in loads:
        load.start()
    z_first(za, za_s, za_r)
    select_a(0)
    x_send(0, 0)
    for yr in (1, 2, 3):
        y_wait(0, yr)
        x_send(0, yr)
    z_first(zb, zb_s, zb_r)
    x_forward(0, 0)
    select_b(0)
    z_second(za, za_s, za_r)
    select_a(1)
    x_send(1, 0)
    x_forward(0, 1)
    x_forward(0, 2)
    x_forward(0, 3)
    for yr in (1, 2, 3):
        y_wait(1, yr)
        x_send(1, yr)
    b_wait(0, 1)
    b_wait(0, 2)
    b_wait(0, 3)
    z_second(zb, zb_s, zb_r)
    select_b(1)
    for load in loads:
        load.wait()
    x_far(0, 0)
    x_far(0, 1)
    sib_wait(0)
    up(0)
    x_far(0, 2)
    x_far(0, 3)
    sib_wait(1)
    up(1)
    x_forward(1, 0)
    x_forward(1, 1)
    x_forward(1, 2)
    h_forward(0)
    down(0)
    x_forward(1, 3)
    h_forward(1)
    down(1)
    b_wait(1, 1)
    b_wait(1, 2)
    b_wait(1, 3)
    x_far(1, 0)
    x_far(1, 1)
    sib_wait(2)
    up(2)
    x_far(1, 2)
    x_far(1, 3)
    sib_wait(3)
    up(3)

    for d in (1, 3, 2):
        arrived(xi.at[(x + d) % NX], xi_s.at[d], xi_r.at[d])
    weights = xi[...].reshape(NX * TOK, 128)
    high = weights.astype(jnp.bfloat16)
    low = (weights - high.astype(jnp.float32)).astype(jnp.bfloat16)
    q = lax.broadcasted_iota(jnp.int32, (128, 512), 0)
    m = lax.broadcasted_iota(jnp.int32, (128, 512), 1)
    spread = (q == (m // 16) * CAP + m % CAP).astype(jnp.bfloat16)
    tr = lax.broadcasted_iota(jnp.int32, (32, 512), 0)
    tc = lax.broadcasted_iota(jnp.int32, (32, 512), 1)
    keep = tr // TOK == (tc // CAP) % NX
    wide = jnp.concatenate(
        [
            jnp.where(keep, jnp.dot(part, spread, preferred_element_type=jnp.float32), 0.0)
            for part in (high, low)
        ],
        axis=0,
    ).astype(jnp.bfloat16)

    h_forward(2)
    down(2)
    h_forward(3)
    down(3)
    for yr in range(NY):
        for slot in range(NZ):
            if yr or slot:
                source = ((y - YREL[yr]) % NY) * NZ + (z - ZREL[slot]) % NZ
                arrived(rb.at[source], r_s.at[yr, slot], r_r.at[yr, slot])
    back = rb[...].reshape(512, OUTS)
    mixed = jnp.dot(wide, back, preferred_element_type=jnp.float32)
    fs[...] = (mixed[: NX * TOK] + mixed[NX * TOK :]).reshape(NX, TOK, OUTS)
    fb[x] = fs[x]
    for d in (1, 3, 2):
        send(fs.at[(x + d) % NX], fb.at[x], f_s.at[d], f_r.at[4 - d], dev(dx=d))
    for d in (1, 3, 2):
        arrived(fb.at[(x + d) % NX], f_s.at[d], f_r.at[d])
    for g in range(NX):
        cols = slice(g * OUTS, (g + 1) * OUTS)
        out_ref[:, cols] = (hid[:, cols] + fb[g]).astype(jnp.bfloat16)
    for copy in sends:
        copy.wait_send()


def on_device(residual, attn_part, norm_gain, routes, gates, gate_weight, up_weight, down_weight):
    bf16, f32 = jnp.bfloat16, jnp.float32
    dma = pltpu.SemaphoreType.DMA
    vmem = pl.BlockSpec(memory_space=pltpu.VMEM)
    hbm = pl.BlockSpec(memory_space=pl.ANY)
    return pl.pallas_call(
        kernel,
        out_shape=jax.ShapeDtypeStruct((TOK, HALF), bf16),
        in_specs=[hbm] * 8,
        out_specs=vmem,
        scratch_shapes=[
            pltpu.VMEM((TOK, HALF), bf16),
            pltpu.VMEM((TOK, D), bf16),
            pltpu.VMEM((HALF // 128, 128), f32),
            pltpu.VMEM((TOK, TOK), jnp.int32),
            pltpu.VMEM((TOK, TOK), f32),
            pltpu.VMEM((D, FFS), bf16),
            pltpu.VMEM((D, FFS), bf16),
            pltpu.VMEM((8 * FFS, OUTS), bf16),
            pltpu.VMEM((2, 16, HALF + QUART), bf16),
            pltpu.VMEM((TOK, HALF), f32),
            pltpu.VMEM((NZ, 16, UA + 128), bf16),
            pltpu.VMEM((NZ, NX, 16, UB + 128), bf16),
            pltpu.VMEM((NX, TOK, 128), f32),
            pltpu.VMEM((2, NY, 16, CA), bf16),
            pltpu.VMEM((2, NY, NX, 16, CB), bf16),
            pltpu.VMEM((2, 2, NY, NX, 16, HALF), bf16),
            pltpu.VMEM((ROWS, 2 * FFS), f32),
            pltpu.VMEM((4, 8, ROWS, FFS), bf16),
            pltpu.VMEM((ROWS, OUTS), f32),
            pltpu.VMEM((2, NY, 4, 16, OUTS), bf16),
            pltpu.VMEM((32, 16, OUTS), bf16),
            pltpu.VMEM((NX, TOK, OUTS), f32),
            pltpu.VMEM((NX, TOK, OUTS), f32),
            dma((5,)),
            dma((3,)),
            dma((1,)),
            dma((1,)),
            dma((NZ,)),
            dma((NZ,)),
            dma((NZ,)),
            dma((NZ,)),
            dma((NX,)),
            dma((NX,)),
            dma((NX,)),
            dma((NX,)),
            dma((2, NY)),
            dma((2, NY)),
            dma((2, NY)),
            dma((2, NY)),
            dma((2, NY, 2)),
            dma((2, NY, 2)),
            dma((2, NY, 2)),
            dma((2, NY, 2)),
            dma((2, NY, 5)),
            dma((2, NY, 5)),
            dma((4, NX)),
            dma((4, NX)),
            dma((4, NX)),
            dma((4, NX)),
            dma((NY, NZ)),
            dma((NY, NZ)),
            dma((NX,)),
            dma((NX,)),
        ],
        compiler_params=pltpu.CompilerParams(
            collective_id=0, has_side_effects=True, vmem_limit_bytes=60 * 2**20
        ),
    )(
        residual,
        attn_part,
        norm_gain.reshape(HALF // 128, 128),
        routes,
        gates,
        gate_weight,
        up_weight,
        down_weight,
    )


def solution(mesh):
    placed = (
        P(("req", "grp"), "head"),
        P("head", ("req", "grp"), None),
        P("head"),
        P(("req", "grp"), None),
        P(("req", "grp"), None),
        P("req", None, ("head", "grp")),
        P("req", None, ("head", "grp")),
        P("req", None, ("head", "grp")),
    )
    return jax.shard_map(
        on_device, mesh=mesh, in_specs=placed, out_specs=P(("req", "grp"), "head"), check_vma=False
    )
```
